128 devices in a mesh: leaf: 32 (over z, y, x_lo), blk: 4 (over x_hi, core).
Axes of the slice: x: 4 (x_hi: 2, x_lo: 2; x = x_hi * 2 + x_lo), y: 4, z: 4, core: 2. Of those that a mesh axis runs over, the one named last changes fastest.
Arguments:
- noise_root: float32 [4096, 512], P('blk'), may hold values from -6 to 6
- block_root: bfloat16 [4096, 4096], P('leaf', 'blk'), as said below
- noise_first: float32 [2048, 1024], P('blk', 'leaf'), may hold values from -6 to 6
- block_first: bfloat16 [4096, 2048], P('leaf', 'blk'), as said below
- coupling_first: bfloat16 [6144, 2048], P('leaf', 'blk'), may hold values from -0.109375 to 0.109375
- structure_first: int32 [6144], P('leaf'), may hold values from 0 to 4095, as said below
- noise_second: float32 [2048, 2048], P('blk', 'leaf'), may hold values from -6 to 6
- block_second: bfloat16 [8192, 2048], P('leaf', 'blk'), as said below
- coupling_second: bfloat16 [12288, 2048], P('leaf', 'blk'), may hold values from -0.109375 to 0.109375
- structure_second: int32 [12288], P('leaf'), may hold values from 0 to 6143, as said below
- noise_third: float32 [1024, 4096], P('blk', 'leaf'), may hold values from -6 to 6
- block_third: bfloat16 [8192, 1024], P('leaf', 'blk'), as said below
- coupling_third: bfloat16 [24576, 1024], P('leaf', 'blk'), may hold values from -0.109375 to 0.109375
- structure_third: int32 [24576], P('leaf'), may hold values from 0 to 8191, as said below
Outputs:
- solved_root: bfloat16 [4096, 512], P(('leaf', 'blk'))
- solved_first: bfloat16 [4096, 512], P(('leaf', 'blk'))
- solved_second: bfloat16 [8192, 512], P(('leaf', 'blk'))
- solved_third: bfloat16 [8192, 512], P(('leaf', 'blk'))
The draws below stay inside these ranges and needn't reach their ends.
Inputs may be any that keep to these rules, and one draw needn't show every extreme that they name: `structure_first`: for each first-level supernode, its 3072 entries are distinct, ascending, and include 0 and 4095. `structure_second`: for each second-level supernode, its 3072 entries are distinct, ascending, and include 0 and 6143. `structure_third`: for each third-level supernode, its 3072 entries are distinct, ascending, and include 0 and 8191. `block_root`: tiles above the diagonal tiles are zero; diagonal tiles are lower triangular with positive diagonals. `block_first`: in each supernode's square block, tiles above the diagonal tiles are zero; diagonal tiles are lower triangular with positive diagonals. `block_second`: in each supernode's square block, tiles above the diagonal tiles are zero; diagonal tiles are lower triangular with positive diagonals. `block_third`: in each supernode's square block, tiles above the diagonal tiles are zero; diagonal tiles are lower triangular with positive diagonals.
All inputs are finite; a program needn't handle non-finite values.
Results may differ from the reference program's by a relative error of at most 0.012.
Values may be sent and summed in bfloat16 or wider, within the bound.
No kernel may reach another device: no remote copies, remote signals or barrier semaphores. Data moves between devices by JAX's collectives and lax.ppermute only.
A program may use at most 128 MiB of HBM per device.

```python
import math
import jax
import jax.numpy as jnp
from jax import lax

SAMPLES = 512
SEP_ROOT = 4096
SEP_FIRST = 2048
SEP_SECOND = 2048
SEP_THIRD = 1024
STRUCT_ROWS = 3072
TILE_ROOT = 1024
TILE_FIRST = 512
TILE_SECOND = 512
TILE_THIRD = 256
ANCESTORS_FIRST = 4096
ANCESTORS_SECOND = 6144
ANCESTORS_THIRD = 8192


def draw_block(key, count, sep_rows, tile_rows):
    key_off, key_low, key_diag = jax.random.split(key, 3)
    row_total = count * sep_rows
    row_index = jnp.arange(row_total)[:, None] % sep_rows
    col_index = jnp.arange(sep_rows)[None, :]
    row_tile = row_index // tile_rows
    col_tile = col_index // tile_rows
    array_shape = (row_total, sep_rows)
    off_values = jnp.clip(jax.random.normal(key_off, array_shape, jnp.float32), -4.0, 4.0) * (0.5 / math.sqrt(sep_rows))
    low_values = jnp.clip(jax.random.normal(key_low, array_shape, jnp.float32), -4.0, 4.0) * (0.5 / math.sqrt(tile_rows))
    diag_values = jax.random.uniform(key_diag, array_shape, jnp.float32, 0.7, 1.4)
    inside = jnp.where(row_index > col_index, low_values, jnp.where(row_index == col_index, diag_values, 0.0))
    values = jnp.where(row_tile > col_tile, off_values, jnp.where(row_tile == col_tile, inside, 0.0))
    return values.astype(jnp.bfloat16)


def draw_rows(key, count, ancestor_rows, struct_rows):
    keys_all = jax.random.split(key, count)

    def single(one_key):
        chosen = jax.random.permutation(one_key, ancestor_rows - 2)[:struct_rows - 2].astype(jnp.int32) + 1
        boundary = jnp.array([0, ancestor_rows - 1], dtype=jnp.int32)
        return jnp.sort(jnp.concatenate([boundary, chosen]))
    return jax.vmap(single)(keys_all).reshape(-1).astype(jnp.int32)


def draw_block_root(key, part):
    return draw_block(key, 1, SEP_ROOT, TILE_ROOT)


def draw_block_first(key, part):
    return draw_block(key, 2, SEP_FIRST, TILE_FIRST)


def draw_block_second(key, part):
    return draw_block(key, 4, SEP_SECOND, TILE_SECOND)


def draw_block_third(key, part):
    return draw_block(key, 8, SEP_THIRD, TILE_THIRD)


def draw_structure_first(key, part):
    return draw_rows(key, 2, ANCESTORS_FIRST, STRUCT_ROWS)


def draw_structure_second(key, part):
    return draw_rows(key, 4, ANCESTORS_SECOND, STRUCT_ROWS)


def draw_structure_third(key, part):
    return draw_rows(key, 8, ANCESTORS_THIRD, STRUCT_ROWS)


def shard_levels(stream_key, shape, cuts, low, top_value):
    def one(dim, shards_of):
        draws = jax.random.uniform(jax.random.fold_in(jax.random.fold_in(stream_key, 6), dim), (shards_of,), jnp.float32, low / len(cuts), top_value / len(cuts))
        return jnp.repeat(jnp.exp(draws), shape[dim] // shards_of).reshape((-1,) + (1,) * (len(shape) - dim - 1))

    factor_of = one(*cuts[0])
    for cut in cuts[1:]:
        factor_of = factor_of * one(*cut)
    return factor_of


def centred(stream_key, dims, scale, reach, cuts=(), kind=jnp.bfloat16):
    gain = shard_levels(stream_key, dims, cuts, -0.22, 0.18) if cuts else 1.0
    values = jax.random.normal(stream_key, dims, jnp.float32) * scale * gain
    return jnp.minimum(jnp.maximum(values, -reach), reach).astype(kind)


def setup_inputs(seed: int = 0) -> dict:
    keys = jax.random.split(jax.random.key(seed), 15)
    noise_root = centred(keys[0], (SEP_ROOT, SAMPLES), 1.0, 6.0, ((0, 4),), jnp.float32)
    block_root = draw_block_root(jax.random.fold_in(keys[14], 71), 0)
    noise_first = centred(keys[2], (SEP_FIRST, 2 * SAMPLES), 1.0, 6.0, ((0, 4), (1, 32)), jnp.float32)
    block_first = draw_block_first(jax.random.fold_in(keys[14], 71), 0)
    coupling_first = centred(keys[4], (2 * STRUCT_ROWS, SEP_FIRST), STRUCT_ROWS ** -0.5, 0.109375, ((0, 32), (1, 4)))
    structure_first = draw_structure_first(jax.random.fold_in(keys[14], 71), 0)
    noise_second = centred(keys[6], (SEP_SECOND, 4 * SAMPLES), 1.0, 6.0, ((0, 4), (1, 32)), jnp.float32)
    block_second = draw_block_second(jax.random.fold_in(keys[14], 71), 0)
    coupling_second = centred(keys[8], (4 * STRUCT_ROWS, SEP_SECOND), STRUCT_ROWS ** -0.5, 0.109375, ((0, 32), (1, 4)))
    structure_second = draw_structure_second(jax.random.fold_in(keys[14], 71), 0)
    noise_third = centred(keys[10], (SEP_THIRD, 8 * SAMPLES), 1.0, 6.0, ((0, 4), (1, 32)), jnp.float32)
    block_third = draw_block_third(jax.random.fold_in(keys[14], 71), 0)
    coupling_third = centred(keys[12], (8 * STRUCT_ROWS, SEP_THIRD), STRUCT_ROWS ** -0.5, 0.109375, ((0, 32), (1, 4)))
    structure_third = draw_structure_third(jax.random.fold_in(keys[14], 71), 0)
    return dict(noise_root=noise_root, block_root=block_root, noise_first=noise_first, block_first=block_first, coupling_first=coupling_first, structure_first=structure_first, noise_second=noise_second, block_second=block_second, coupling_second=coupling_second, structure_second=structure_second, noise_third=noise_third, block_third=block_third, coupling_third=coupling_third, structure_third=structure_third)


def transposed_product(left, right):
    return lax.dot_general(left, right, (((0,), (0,)), ((), ())), preferred_element_type=jnp.float32)


def backward_supernode(factor_block, residual, tile_rows):
    count = factor_block.shape[0] // tile_rows
    solution = [None] * count
    for target in reversed(range(count)):
        first_row = target * tile_rows
        lower_row = first_row + tile_rows
        right_side = residual[first_row:lower_row]
        if target < count - 1:
            later = jnp.concatenate(solution[target + 1:], 0)
            right_side = right_side - transposed_product(factor_block[lower_row:, first_row:lower_row], later)
        inverse = factor_block[first_row:lower_row, first_row:lower_row]
        solution[target] = transposed_product(inverse, right_side.astype(jnp.bfloat16)).astype(jnp.bfloat16)
    return jnp.concatenate(solution, 0)


def reference(noise_root, block_root, noise_first, block_first, coupling_first, structure_first,
              noise_second, block_second, coupling_second, structure_second,
              noise_third, block_third, coupling_third, structure_third):
    levels_data = [
        (noise_root, block_root, None, None, SEP_ROOT, TILE_ROOT),
        (noise_first, block_first, coupling_first, structure_first, SEP_FIRST, TILE_FIRST),
        (noise_second, block_second, coupling_second, structure_second, SEP_SECOND, TILE_SECOND),
        (noise_third, block_third, coupling_third, structure_third, SEP_THIRD, TILE_THIRD),
    ]
    levels_solved = []
    for level_number, (noise, stacked, coupling, structure, sep_rows, tile_rows) in enumerate(levels_data):
        results = []
        for group_index in range(2 ** level_number):
            factor_block = stacked[group_index * sep_rows:(group_index + 1) * sep_rows]
            if level_number == 0:
                residual = noise
            else:
                pieces = []
                for earlier in range(level_number):
                    earlier_rows = levels_solved[earlier].shape[0] // (2 ** earlier)
                    owner = group_index >> (level_number - earlier)
                    pieces.append(levels_solved[earlier][owner * earlier_rows:(owner + 1) * earlier_rows])
                ancestors = jnp.concatenate(pieces, 0)
                rows_list = structure[group_index * STRUCT_ROWS:(group_index + 1) * STRUCT_ROWS]
                picked = jnp.take(ancestors, rows_list, axis=0)
                own_coupling = coupling[group_index * STRUCT_ROWS:(group_index + 1) * STRUCT_ROWS]
                residual = noise[:, group_index * SAMPLES:(group_index + 1) * SAMPLES] - transposed_product(own_coupling, picked)
            results.append(backward_supernode(factor_block, residual, tile_rows))
        levels_solved.append(jnp.concatenate(results, 0))
    return (levels_solved[0], levels_solved[1], levels_solved[2], levels_solved[3])
```

```python
import jax
import jax.numpy as jnp
from jax import lax
from jax.sharding import Mesh, PartitionSpec as P

BF = jnp.bfloat16
F32 = jnp.float32
AXES = ("z1", "z0", "y1", "y0", "x0", "x1", "c")
LEAF = ("z1", "z0", "y1", "y0", "x0")
BLK = ("x1", "c")
SIDE = ("y0", "x0")
TEAM = ("y0", "x0", "x1", "c")
FIRST = ("z0", "y1", "y0", "x0")
SECOND = ("y1", "y0", "x0")


def dot(left, right):
    return lax.dot_general(left, right, (((1,), (0,)), ((), ())), preferred_element_type=F32)


def swap(array, axes, bits, keep=None):
    count = lax.axis_size(axes)
    route = [(i, i ^ bits) for i in range(count) if keep is None or keep(i)]
    return lax.ppermute(array, axes, route)


def pair_stack(array, axis, at=0):
    other = swap(array, axis, 1)
    low = lax.axis_index(axis) == 0
    return jnp.stack([jnp.where(low, array, other), jnp.where(low, other, array)], at)


def quad_stack(array, axes):
    me = lax.axis_index(axes)
    pieces = [array] + [swap(array, axes, bits) for bits in (1, 2, 3)]
    odd = (me & 1) == 1
    high = (me & 2) == 2
    a, b, c, d = pieces
    a, b = jnp.where(odd, b, a), jnp.where(odd, a, b)
    c, d = jnp.where(odd, d, c), jnp.where(odd, c, d)
    return jnp.stack([jnp.where(high, c, a), jnp.where(high, d, b), jnp.where(high, a, c), jnp.where(high, b, d)], 0)


def team_gather(part):
    copies = jnp.broadcast_to(part[None], (16,) + part.shape)
    return lax.all_to_all(copies, TEAM, 0, 0, tiled=True).reshape(16 * part.shape[0], part.shape[1])


def pick(x_t, idx, offset, total, first_entry=0):
    entries = idx.shape[0]
    slack = total - entries
    step = 512
    out = []
    for start in range(0, entries, step):
        low = max(start, offset) - offset
        high = min(start + step + slack, offset + x_t.shape[1]) - offset
        if high <= low:
            out.append(jnp.zeros((x_t.shape[0], step), F32))
            continue
        rows = lax.broadcasted_iota(jnp.int32, (high - low, step), 0) + (low + offset)
        hot = (rows == idx[start : start + step][None, :]).astype(BF)
        out.append(dot(x_t[:, low:high], hot))
    return jnp.concatenate(out, 1)


def solve_root(noise_root, block_root):
    z = lax.axis_index(("z1", "z0"))
    z1, z0, y1 = (lax.axis_index(a) for a in ("z1", "z0", "y1"))
    y0, x0 = lax.axis_index("y0"), lax.axis_index("x0")
    blk = lax.axis_index(BLK)
    member = lax.axis_index(TEAM)
    sample0 = (z0 * 4 + y1 * 2 + z1) * 64
    block_t = block_root.T
    got = lax.all_to_all(block_t, TEAM, 0, 0, tiled=True)
    got = got.reshape(4, 4, 64, 128).transpose(1, 2, 0, 3).reshape(256, 512)
    both = pair_stack(got, "y1", 1).reshape(256, 1024)
    ring = [both] + [swap(both, ("z1", "z0"), bits) for bits in (1, 2, 3)]
    odd = (z & 1) == 1
    high = (z & 2) == 2
    a, b, c, d = ring
    a, b = jnp.where(odd, b, a), jnp.where(odd, a, b)
    c, d = jnp.where(odd, d, c), jnp.where(odd, c, d)
    tiles = [jnp.where(high, c, a), jnp.where(high, d, b), jnp.where(high, a, c), jnp.where(high, b, d)]
    mine = lax.dynamic_slice_in_dim(noise_root, sample0, 64, 1)
    lead = jnp.where(blk == 3, mine.astype(BF), jnp.zeros(mine.shape, BF))
    right = lead
    for bits in (1, 2, 3):
        right = right + swap(lead, BLK, bits, lambda i: i == 3)
    team_rows = mine.reshape(4, 4, 64, 64)
    team_rows = lax.dynamic_index_in_dim(team_rows, y0 * 2 + x0, 0, False)
    pieces = []
    for bits in (0, 1, 2, 3):
        piece = lax.dynamic_index_in_dim(team_rows, blk ^ bits, 0, False)
        pieces.append(piece if bits == 0 else swap(piece, BLK, bits))
    pieces = jnp.stack(pieces, 0)
    noise_part = [lax.dynamic_index_in_dim(pieces, blk ^ t, 0, False) for t in range(4)]
    solved = [None] * 4
    acc = None
    for t in (3, 2, 1, 0):
        if t < 3:
            part = (noise_part[t] - acc[t * 64 : (t + 1) * 64]).astype(BF)
            right = team_gather(part)
        x_part = dot(tiles[t][t * 64 : (t + 1) * 64], right).astype(BF)
        solved[t] = team_gather(x_part)
        if t:
            more = dot(tiles[t][: t * 64], solved[t])
            acc = more if acc is None else acc[: t * 64] + more
    return jnp.concatenate(solved, 0)


def solve_chain(block, residual, tile):
    blk = lax.axis_index(BLK)
    inverse = lax.dynamic_slice_in_dim(block, blk * tile, tile, 0)
    right = residual
    solved = [None] * 4
    for t in (3, 2, 1, 0):
        own = dot(right.astype(BF), inverse).astype(BF)
        own = jnp.where(blk == t, own, jnp.zeros(own.shape, BF))
        full = own
        for bits in (1, 2, 3):
            full = full + swap(own, BLK, bits, lambda i: i == t)
        solved[t] = full
        if t:
            right = right - dot(full, block[t * tile : (t + 1) * tile])
    return jnp.concatenate(solved, 1)


def local(noise_root, block_root, noise_first, block_first, coupling_first, structure_first,
          noise_second, block_second, coupling_second, structure_second,
          noise_third, block_third, coupling_third, structure_third):
    z1, z0, y1, y0, x0 = (lax.axis_index(a) for a in LEAF)
    blk = lax.axis_index(BLK)

    lists = jnp.concatenate([structure_first, structure_second, structure_third])
    lists = quad_stack(lists[None], SIDE)[:, 0]
    idx_third = lists[:, 576:].reshape(3072)
    upper = pair_stack(lists[:, :576], "y1")
    idx_second = upper[:, :, 192:].reshape(3072)
    idx_first = pair_stack(upper[:, :, :192], "z0").reshape(3072)

    full_first = lax.all_gather(block_first, FIRST, axis=0, tiled=True)
    full_second = lax.all_gather(block_second, SECOND, axis=0, tiled=True)
    full_third = quad_stack(block_third, SIDE).reshape(1024, 256)
    coup_first = quad_stack(coupling_first, SIDE)
    coup_first = pair_stack(coup_first, "y1")
    coup_first = pair_stack(coup_first, "z0").reshape(3072, 512)
    coup_second = lax.all_gather(coupling_second, SECOND, axis=0, tiled=True)
    coup_third = quad_stack(coupling_third, SIDE).reshape(3072, 256)

    noise1 = noise_first.T
    halves = noise_second.T.reshape(2, 32, 512)
    a = y1
    first_route, second_route = [], []
    for s in range(8):
        p, q, r = s >> 2, s >> 1 & 1, s & 1
        first_route.append((s, q * 4 + r * 2 + p))
        second_route.append((s, q * 4 + r * 2 + 1 - p))
    same = lax.ppermute(lax.dynamic_index_in_dim(halves, a, 0, False), SECOND, first_route)
    cross = lax.ppermute(lax.dynamic_index_in_dim(halves, 1 - a, 0, False), SECOND, second_route)
    noise2 = jnp.concatenate([jnp.where(x0 == 0, same, cross), jnp.where(x0 == 0, cross, same)], 0)
    quarters = noise_third.T.reshape(4, 32, 256)
    me = y0 * 2 + x0
    pieces = []
    for bits in (0, 1, 2, 3):
        piece = lax.dynamic_index_in_dim(quarters, me ^ bits, 0, False)
        pieces.append(piece if bits == 0 else swap(piece, SIDE, bits))
    pieces = jnp.stack(pieces, 0)
    noise3 = jnp.concatenate([lax.dynamic_index_in_dim(pieces, me ^ t, 0, False) for t in range(4)], 0)

    root = solve_root(noise_root, block_root)
    root_t = root.T
    half = lax.dynamic_slice_in_dim(root_t, x0 * 32, 32, 0)
    far = lax.ppermute(half, ("z1", "y0"), [(0, 2), (3, 1)])
    root1 = jnp.where(z1 == y0, half, far)

    res1 = noise1 - dot(pick(root1, idx_first, 0, 4096).astype(BF), coup_first)
    first1 = solve_chain(full_first, res1, 512)
    root2 = pair_stack(root1, "z0").reshape(64, 4096)
    first2 = pair_stack(first1, "z0").reshape(64, 2048)

    picked2 = pick(root2, idx_second, 0, 6144) + pick(first2, idx_second, 4096, 6144)
    res2 = noise2 - dot(picked2.astype(BF), coup_second)
    second2 = solve_chain(full_second, res2, 512)

    def widen(array):
        return pair_stack(array.reshape(2, 32, array.shape[1]), "y1", 1).reshape(128, array.shape[1])

    root3 = widen(root2)
    first3 = widen(first2)
    second3 = widen(second2)

    picked3 = pick(root3, idx_third, 0, 8192) + pick(first3, idx_third, 4096, 8192)
    picked3 = picked3 + pick(second3, idx_third, 6144, 8192)
    res3 = noise3 - dot(picked3.astype(BF), coup_third)
    third3 = solve_chain(full_third, res3, 256)

    def rows_for(array, rows, spread):
        per = array.reshape(array.shape[0], spread, 4, rows)
        per = lax.dynamic_index_in_dim(per, blk, 2, False)
        per = per.transpose(1, 2, 0)
        return jnp.broadcast_to(per[None], (16 // spread,) + per.shape).reshape(16, rows * array.shape[0] // 128, 128)

    own_half = lax.dynamic_slice_in_dim(root1, z1 * 2048, 2048, 1)
    send = jnp.concatenate(
        [rows_for(own_half, 32, 16), rows_for(first1, 32, 16), rows_for(second2, 64, 8), rows_for(third3, 64, 4)], 1
    )
    got = lax.all_to_all(send, FIRST, 0, 0, tiled=True)
    out0 = got[:, :8].reshape(16, 32, 32).transpose(1, 0, 2).reshape(32, 512)
    out1 = got[:, 8:16].reshape(16, 32, 32).transpose(1, 0, 2).reshape(32, 512)
    two = lax.dynamic_slice_in_dim(got[:, 16:48], z0 * 8, 8, 0)
    out2 = two.reshape(8, 64, 2, 32).transpose(1, 2, 0, 3).reshape(64, 512)
    three = lax.dynamic_slice_in_dim(got[:, 48:112], (z0 * 2 + y1) * 4, 4, 0)
    out3 = three.reshape(4, 64, 4, 32).transpose(1, 2, 0, 3).reshape(64, 512)
    return out0, out1, out2, out3


def solution(mesh):
    fine = Mesh(mesh.devices.reshape((2,) * 7), AXES)
    both = P(LEAF, BLK)
    cross = P(BLK, LEAF)
    list_spec = P(LEAF)
    in_specs = (P(BLK, None), both, cross, both, both, list_spec, cross, both, both, list_spec, cross, both, both, list_spec)
    out_specs = (P(LEAF + BLK, None),) * 4
    return jax.shard_map(local, mesh=fine, in_specs=in_specs, out_specs=out_specs, check_vma=False)
```

```python
import jax
import jax.numpy as jnp
from jax import lax
from jax.sharding import Mesh, PartitionSpec as P

BF = jnp.bfloat16
F32 = jnp.float32
AXES = ("z1", "z0", "y1", "y0", "x0", "x1", "c")
LEAF = ("z1", "z0", "y1", "y0", "x0")
BLK = ("x1", "c")
SIDE = ("y0", "x0")
FIRST = ("z0", "y1", "y0", "x0")
SECOND = ("y1", "y0", "x0")


def dot(left, right):
    return lax.dot_general(left, right, (((1,), (0,)), ((), ())), preferred_element_type=F32)


def swap(array, axes, bits, keep=None):
    count = lax.axis_size(axes)
    route = [(i, i ^ bits) for i in range(count) if keep is None or keep(i)]
    return lax.ppermute(array, axes, route)


def pair_stack(array, axis, at=0):
    other = swap(array, axis, 1)
    low = lax.axis_index(axis) == 0
    return jnp.stack([jnp.where(low, array, other), jnp.where(low, other, array)], at)


def quad_stack(array, axes):
    me = lax.axis_index(axes)
    pieces = [array] + [swap(array, axes, bits) for bits in (1, 2, 3)]
    odd = (me & 1) == 1
    high = (me & 2) == 2
    a, b, c, d = pieces
    a, b = jnp.where(odd, b, a), jnp.where(odd, a, b)
    c, d = jnp.where(odd, d, c), jnp.where(odd, c, d)
    return jnp.stack([jnp.where(high, c, a), jnp.where(high, d, b), jnp.where(high, a, c), jnp.where(high, b, d)], 0)


def pick(x_t, idx, offset, total, first_entry=0):
    entries = idx.shape[0]
    slack = total - entries
    step = 512
    out = []
    for start in range(0, entries, step):
        low = max(start, offset) - offset
        high = min(start + step + slack, offset + x_t.shape[1]) - offset
        if high <= low:
            out.append(jnp.zeros((x_t.shape[0], step), F32))
            continue
        rows = lax.broadcasted_iota(jnp.int32, (high - low, step), 0) + (low + offset)
        hot = (rows == idx[start : start + step][None, :]).astype(BF)
        out.append(dot(x_t[:, low:high], hot))
    return jnp.concatenate(out, 1)


def quad_list(array, axes):
    pieces = [array] + [swap(array, axes, bits) for bits in (1, 2, 3)]
    return jnp.stack(pieces, 0)


def root_weights(block_root):
    c = lax.axis_index("c")
    x0 = lax.axis_index("x0")
    halves = block_root.reshape(128, 2, 512)
    kept = lax.dynamic_index_in_dim(halves, x0, 1, False)
    gone = lax.dynamic_index_in_dim(halves, 1 - x0, 1, False)
    kept = lax.ppermute(kept, ("x0", "c"), [(0, 0), (1, 2), (2, 1), (3, 3)])
    gone = lax.ppermute(gone, ("x0", "c"), [(0, 1), (1, 3), (2, 0), (3, 2)])
    even = jnp.where(c == 0, kept, gone)
    odd = jnp.where(c == 0, gone, kept)
    rows = jnp.concatenate([even, odd], 0)
    left = quad_list(rows[:, :256], ("y1", "y0"))
    right = quad_list(rows[:, 256:], ("z1", "z0"))
    left = quad_list(left, ("z1", "z0"))
    right = quad_list(right, ("y1", "y0"))
    return left, right


def solve_root(noise_root, left, right):
    z = lax.axis_index(("z1", "z0"))
    y = lax.axis_index(("y1", "y0"))
    z1, z0, x0, c = (lax.axis_index(a) for a in ("z1", "z0", "x0", "c"))
    tile = lax.axis_index("x1") * 2 + x0
    sample0 = ((z0 * 4 + y) * 2 + z1) * 32

    def row_tile(u):
        rows = []
        for v in range(4):
            a = lax.dynamic_slice(left, (u ^ z, v ^ y, 0, 0), (1, 1, 256, 256))
            b = lax.dynamic_slice(right, (v ^ y, u ^ z, 0, 0), (1, 1, 256, 256))
            rows.append(jnp.concatenate([a.reshape(256, 256), b.reshape(256, 256)], 1))
        return jnp.concatenate(rows, 0)

    def share(half):
        other = swap(half, "c", 1)
        return jnp.concatenate([jnp.where(c == 0, half, other), jnp.where(c == 0, other, half)], 1)

    mine = lax.dynamic_slice_in_dim(noise_root, sample0, 32, 1).T
    held = lax.dynamic_slice_in_dim(mine, c * 512, 512, 1)
    sent = lax.dynamic_slice_in_dim(mine, (1 - c) * 512, 512, 1)
    rest = jnp.where(c == x0, held, swap(sent, "c", 1))
    diagonal = row_tile(tile)
    solved = [None] * 4
    for t in (3, 2, 1, 0):
        own = dot(share(rest.astype(BF)), diagonal).astype(BF)
        own = jnp.where(tile == t, own, jnp.zeros(own.shape, BF))
        half = own
        for bits in (1, 2, 3):
            half = half + swap(own, ("x0", "x1"), bits, lambda i: i == (t & 1) * 2 + (t >> 1))
        solved[t] = share(half)
        if t:
            rest = rest - dot(solved[t], row_tile(t))
    return jnp.concatenate(solved, 1)


def solve_chain(block, residual, tile):
    blk = lax.axis_index(BLK)
    inverse = lax.dynamic_slice_in_dim(block, blk * tile, tile, 0)

    def own(t, rest):
        value = dot(rest.astype(BF), inverse).astype(BF)
        return jnp.where(blk == t, value, jnp.zeros(value.shape, BF))

    def send(value, *route):
        return lax.ppermute(value, BLK, list(route))

    def times(value, t):
        return dot(value, block[t * tile : (t + 1) * tile])

    rest = residual
    s3 = own(3, rest)
    near3 = s3 + send(s3, (3, 2))
    far3 = send(near3, (3, 1), (2, 0))
    rest = rest - times(near3, 3)
    s2 = own(2, rest)
    near2 = send(s2, (2, 3))
    far2 = send(s2, (2, 1)) + send(s2, (2, 0))
    rest = rest - times(far3, 3)
    rest = rest - times(far2, 2)
    s1 = own(1, rest)
    near1 = s1 + send(s1, (1, 0))
    far1 = send(near1, (1, 3), (0, 2))
    rest = rest - times(near1, 1)
    s0 = own(0, rest)
    full0 = s0 + send(s0, (0, 1)) + send(s0, (0, 2)) + send(s0, (0, 3))
    return jnp.concatenate([full0, near1 + far1, s2 + near2 + far2, near3 + far3], 1)


def local(noise_root, block_root, noise_first, block_first, coupling_first, structure_first,
          noise_second, block_second, coupling_second, structure_second,
          noise_third, block_third, coupling_third, structure_third):
    z1, z0, y1, y0, x0 = (lax.axis_index(a) for a in LEAF)
    blk = lax.axis_index(BLK)

    left, right = root_weights(block_root)
    (coupling_first, block_second, block_third, coupling_third, lists), left, right = lax.optimization_barrier(
        ((coupling_first, block_second, block_third, coupling_third,
          jnp.concatenate([structure_first, structure_second, structure_third])), left, right)
    )

    lists = quad_stack(lists[None], SIDE)[:, 0]
    idx_third = lists[:, 576:].reshape(3072)
    upper = pair_stack(lists[:, :576], "y1")
    idx_second = upper[:, :, 192:].reshape(3072)
    idx_first = pair_stack(upper[:, :, :192], "z0").reshape(3072)

    full_first = lax.all_gather(block_first, FIRST, axis=0, tiled=True)
    coup_second = lax.all_gather(coupling_second, SECOND, axis=0, tiled=True)
    coup_first = quad_stack(coupling_first, SIDE)
    coup_first = pair_stack(coup_first, "y1")
    coup_first = pair_stack(coup_first, "z0").reshape(3072, 512)
    coup_first, block_second, block_third, coupling_third = lax.optimization_barrier(
        (coup_first, block_second, block_third, coupling_third)
    )
    full_second = pair_stack(quad_stack(block_second, SIDE), "y1").reshape(2048, 512)
    full_third = quad_stack(block_third, SIDE).reshape(1024, 256)
    coup_third = quad_stack(coupling_third, SIDE).reshape(3072, 256)

    noise1 = noise_first.T
    halves = noise_second.T.reshape(2, 32, 512)
    a = y1
    first_route, second_route = [], []
    for s in range(8):
        p, q, r = s >> 2, s >> 1 & 1, s & 1
        first_route.append((s, q * 4 + r * 2 + p))
        second_route.append((s, q * 4 + r * 2 + 1 - p))
    same = lax.ppermute(lax.dynamic_index_in_dim(halves, a, 0, False), SECOND, first_route)
    cross = lax.ppermute(lax.dynamic_index_in_dim(halves, 1 - a, 0, False), SECOND, second_route)
    noise2 = jnp.concatenate([jnp.where(x0 == 0, same, cross), jnp.where(x0 == 0, cross, same)], 0)
    quarters = noise_third.T.reshape(4, 32, 256)
    me = y0 * 2 + x0
    pieces = []
    for bits in (0, 1, 2, 3):
        piece = lax.dynamic_index_in_dim(quarters, me ^ bits, 0, False)
        pieces.append(piece if bits == 0 else swap(piece, SIDE, bits))
    pieces = jnp.stack(pieces, 0)
    noise3 = jnp.concatenate([lax.dynamic_index_in_dim(pieces, me ^ t, 0, False) for t in range(4)], 0)

    root = solve_root(noise_root, left, right)
    far = lax.ppermute(root, ("z1", "x0"), [(0, 2), (3, 1)])
    root1 = jnp.where(z1 == x0, root, far)

    res1 = noise1 - dot(pick(root1, idx_first, 0, 4096).astype(BF), coup_first)
    first1 = solve_chain(full_first, res1, 512)
    root2 = pair_stack(root1, "z0").reshape(64, 4096)
    first2 = pair_stack(first1, "z0").reshape(64, 2048)

    picked2 = pick(root2, idx_second, 0, 6144) + pick(first2, idx_second, 4096, 6144)
    res2 = noise2 - dot(picked2.astype(BF), coup_second)
    second2 = solve_chain(full_second, res2, 512)

    def widen(array):
        return pair_stack(array.reshape(2, 32, array.shape[1]), "y1", 1).reshape(128, array.shape[1])

    root3 = widen(root2)
    first3 = widen(first2)
    second3 = widen(second2)

    picked3 = pick(root3, idx_third, 0, 8192) + pick(first3, idx_third, 4096, 8192)
    picked3 = picked3 + pick(second3, idx_third, 6144, 8192)
    res3 = noise3 - dot(picked3.astype(BF), coup_third)
    third3 = solve_chain(full_third, res3, 256)

    def rows_for(array, rows, spread):
        per = array.reshape(array.shape[0], spread, 4, rows)
        per = lax.dynamic_index_in_dim(per, blk, 2, False)
        per = per.transpose(1, 2, 0)
        return per.reshape(spread, rows * array.shape[0] // 128, 128)

    own_half = lax.dynamic_slice_in_dim(root1, z1 * 2048, 2048, 1)
    send = jnp.concatenate([rows_for(own_half, 32, 16), rows_for(first1, 32, 16)], 1)
    got = lax.all_to_all(send, FIRST, 0, 0, tiled=True)
    out0 = got[:, :8].reshape(16, 32, 32).transpose(1, 0, 2).reshape(32, 512)
    out1 = got[:, 8:16].reshape(16, 32, 32).transpose(1, 0, 2).reshape(32, 512)
    two = lax.all_to_all(rows_for(second2, 64, 8), SECOND, 0, 0, tiled=True)
    out2 = two.reshape(8, 64, 2, 32).transpose(1, 2, 0, 3).reshape(64, 512)
    three = lax.all_to_all(rows_for(third3, 64, 4), SIDE, 0, 0, tiled=True)
    out3 = three.reshape(4, 64, 4, 32).transpose(1, 2, 0, 3).reshape(64, 512)
    return out0, out1, out2, out3


def solution(mesh):
    fine = Mesh(mesh.devices.reshape((2,) * 7), AXES)
    both = P(LEAF, BLK)
    cross = P(BLK, LEAF)
    list_spec = P(LEAF)
    in_specs = (P(BLK, None), both, cross, both, both, list_spec, cross, both, both, list_spec, cross, both, both, list_spec)
    out_specs = (P(LEAF + BLK, None),) * 4
    return jax.shard_map(local, mesh=fine, in_specs=in_specs, out_specs=out_specs, check_vma=False)
```

```python
import jax
import jax.numpy as jnp
from jax import lax
from jax.sharding import Mesh, PartitionSpec as P

BF = jnp.bfloat16
F32 = jnp.float32
AXES = ("z1", "z0", "y1", "y0", "x0", "x1", "c")
LEAF = ("z1", "z0", "y1", "y0", "x0")
BLK = ("x1", "c")
SIDE = ("y0", "x0")
FIRST = ("z0", "y1", "y0", "x0")
SECOND = ("y1", "y0", "x0")


def dot(left, right):
    return lax.dot_general(left, right, (((1,), (0,)), ((), ())), preferred_element_type=F32)


def swap(array, axes, bits, keep=None):
    count = lax.axis_size(axes)
    route = [(i, i ^ bits) for i in range(count) if keep is None or keep(i)]
    return lax.ppermute(array, axes, route)


def pair_stack(array, axis, at=0):
    other = swap(array, axis, 1)
    low = lax.axis_index(axis) == 0
    return jnp.stack([jnp.where(low, array, other), jnp.where(low, other, array)], at)


def pick(x_t, idx, offset, total, first_entry=0):
    entries = idx.shape[0]
    slack = total - entries
    step = 512
    out = []
    for start in range(0, entries, step):
        low = max(start, offset) - offset
        high = min(start + step + slack, offset + x_t.shape[1]) - offset
        if high <= low:
            out.append(jnp.zeros((x_t.shape[0], step), F32))
            continue
        rows = lax.broadcasted_iota(jnp.int32, (high - low, step), 0) + (low + offset)
        hot = (rows == idx[start : start + step][None, :]).astype(BF)
        out.append(dot(x_t[:, low:high], hot))
    return jnp.concatenate(out, 1)


def bulk_gather(array, axes):
    count = lax.axis_size(axes)
    copies = jnp.broadcast_to(array[None], (count,) + array.shape)
    return lax.all_to_all(copies, axes, 0, 0, tiled=True)


def coupled(picked, coupling, axes):
    count = lax.axis_size(axes)
    rows, tile = coupling.shape
    samples = picked.shape[0]
    send = picked.astype(BF).reshape(samples, count, rows).transpose(1, 0, 2)
    got = lax.all_to_all(send, axes, 0, 0, tiled=True).reshape(count * samples, rows)
    part = dot(got, coupling).astype(BF).reshape(count, samples, tile)
    back = lax.all_to_all(part, axes, 0, 0, tiled=True)
    return jnp.sum(back.astype(F32), 0)


class Beside:
    def __init__(self, arrays, stages):
        self.arrays = arrays
        self.stages = list(stages)

    def step(self, value):
        if self.stages:
            stage = self.stages.pop(0)
            if stage is not None:
                value, self.arrays = lax.optimization_barrier((value, self.arrays))
                self.arrays = stage(self.arrays)
        return value


def root_rows(block_root):
    c = lax.axis_index("c")
    x0 = lax.axis_index("x0")
    halves = block_root.reshape(128, 2, 512)
    kept = lax.dynamic_index_in_dim(halves, x0, 1, False)
    gone = lax.dynamic_index_in_dim(halves, 1 - x0, 1, False)
    kept = lax.ppermute(kept, ("x0", "c"), [(0, 0), (1, 2), (2, 1), (3, 3)])
    gone = lax.ppermute(gone, ("x0", "c"), [(0, 1), (1, 3), (2, 0), (3, 2)])
    even = jnp.where(c == 0, kept, gone)
    odd = jnp.where(c == 0, gone, kept)
    rows = jnp.concatenate([even, odd], 0)
    return rows


def solve_root(noise_root, weights):
    y = lax.axis_index(("y1", "y0"))
    z0, x0, c = (lax.axis_index(a) for a in ("z0", "x0", "c"))
    tile = lax.axis_index("x1") * 2 + x0
    sample0 = (z0 * 4 + y) * 64

    def share(half):
        return lax.all_gather(half, "c", axis=1, tiled=True)

    mine = lax.dynamic_slice_in_dim(noise_root, sample0, 64, 1).T
    held = lax.dynamic_slice_in_dim(mine, c * 512, 512, 1)
    sent = lax.dynamic_slice_in_dim(mine, (1 - c) * 512, 512, 1)
    rest = jnp.where(c == x0, held, swap(sent, "c", 1))
    diagonal = lax.dynamic_slice_in_dim(weights, tile * 1024, 1024, 0)
    solved = [None] * 4
    for t in (3, 2, 1, 0):
        own = dot(share(rest.astype(BF)), diagonal).astype(BF)
        own = jnp.where(tile == t, own, jnp.zeros(own.shape, BF))
        half = own
        for bits in (1, 2, 3):
            half = half + swap(own, ("x0", "x1"), bits, lambda i: i == (t & 1) * 2 + (t >> 1))
        solved[t] = share(half)
        if t:
            rest = rest - dot(solved[t], weights[t * 1024 : (t + 1) * 1024])
    return jnp.concatenate(solved, 1)


def solve_chain(block, residual, tile, beside):
    blk = lax.axis_index(BLK)
    x1 = lax.axis_index("x1")
    inverse = lax.dynamic_slice_in_dim(block, blk * tile, tile, 0)
    below = lax.dynamic_slice_in_dim(block, (2 * x1 + 1) * tile, tile, 0)

    def chip_solve(rest):
        rest = beside.step(rest)
        later = lax.all_gather(dot(rest.astype(BF), inverse).astype(BF), "c")[1]
        rest = rest - dot(later, below)
        rest = beside.step(rest)
        sooner = lax.all_gather(dot(rest.astype(BF), inverse).astype(BF), "c")[0]
        return lax.all_gather(jnp.concatenate([sooner, later], 1), "x1")

    late = chip_solve(residual)[1]
    early = chip_solve(residual - dot(late, block[2 * tile :]))[0]
    early = beside.step(early)
    return jnp.concatenate([early, late], 1)


def local(noise_root, block_root, noise_first, block_first, coupling_first, structure_first,
          noise_second, block_second, coupling_second, structure_second,
          noise_third, block_third, coupling_third, structure_third):
    z1, z0, y1, y0, x0 = (lax.axis_index(a) for a in LEAF)
    blk = lax.axis_index(BLK)

    lists = jnp.concatenate([structure_first, structure_second, structure_third])
    for place, axis in enumerate(("z0", "y1", "y0")):
        lists = pair_stack(lists, axis, place)

    def along(axis):
        return lambda pair: tuple(pair_stack(array, axis) for array in pair)

    rows, lists = lax.optimization_barrier((root_rows(block_root), lists))
    weights = bulk_gather(rows, ("z1", "z0", "y1", "y0")).reshape(4096, 512)
    lists = pair_stack(lists, "x0", 3).reshape(16, 1344)
    idx_first = lists[:, :192].reshape(3072)
    idx_second = lax.dynamic_slice(lists, (z0 * 8, 192), (8, 384)).reshape(3072)
    idx_third = lax.dynamic_slice(lists, (z0 * 8 + y1 * 4, 576), (4, 768)).reshape(3072)

    noise1 = noise_first.T
    halves = noise_second.T.reshape(2, 32, 512)
    a = y1
    first_route, second_route = [], []
    for s in range(8):
        p, q, r = s >> 2, s >> 1 & 1, s & 1
        first_route.append((s, q * 4 + r * 2 + p))
        second_route.append((s, q * 4 + r * 2 + 1 - p))
    same = lax.ppermute(lax.dynamic_index_in_dim(halves, a, 0, False), SECOND, first_route)
    cross = lax.ppermute(lax.dynamic_index_in_dim(halves, 1 - a, 0, False), SECOND, second_route)
    noise2 = jnp.concatenate([jnp.where(x0 == 0, same, cross), jnp.where(x0 == 0, cross, same)], 0)
    quarters = noise_third.T.reshape(4, 32, 256)
    me = y0 * 2 + x0
    pieces = []
    for bits in (0, 1, 2, 3):
        piece = lax.dynamic_index_in_dim(quarters, me ^ bits, 0, False)
        pieces.append(piece if bits == 0 else swap(piece, SIDE, bits))
    pieces = jnp.stack(pieces, 0)
    noise3 = jnp.concatenate([lax.dynamic_index_in_dim(pieces, me ^ t, 0, False) for t in range(4)], 0)

    full_first = lax.all_gather(block_first, FIRST, axis=0, tiled=True)
    full_second = lax.all_gather(block_second, SECOND, axis=0, tiled=True)
    ready = (weights, idx_first, idx_second, idx_third, noise1, noise2, noise3)
    weights, idx_first, idx_second, idx_third, noise1, noise2, noise3 = lax.optimization_barrier(ready)

    root = solve_root(noise_root, weights)
    root1 = lax.dynamic_slice_in_dim(root, x0 * 32, 32, 0)

    def widen(array):
        return pair_stack(array.reshape(2, 32, array.shape[1]), "y1", 1).reshape(128, array.shape[1])

    res1 = noise1 - coupled(pick(root1, idx_first, 0, 4096), coupling_first, FIRST)
    root2 = pair_stack(root1, "z0").reshape(64, 4096)
    wide2, res1 = lax.optimization_barrier((root2, res1))
    wide2 = widen(wide2)
    first1 = solve_chain(full_first, res1, 512, Beside((), []))
    wide2, first1 = lax.optimization_barrier((wide2, first1))
    first2 = lax.all_gather(first1, "z0").reshape(64, 2048)

    third_stages = Beside((block_third, coupling_third), [along("x0"), None, along("y0"), None, None, lambda v: v])
    first2 = third_stages.step(first2)
    picked2 = pick(root2, idx_second, 0, 6144) + pick(first2, idx_second, 4096, 6144)
    res2 = noise2 - coupled(picked2, coupling_second, SECOND)
    wide1, res2 = lax.optimization_barrier((first2, res2))
    first3 = widen(wide1)
    second2 = solve_chain(full_second, res2, 512, third_stages)
    first3, second2 = lax.optimization_barrier((first3, second2))
    full_third, coup_third = (array.reshape(-1, 256) for array in third_stages.arrays)

    def rows_for(array, rows, spread):
        per = array.reshape(array.shape[0], spread, 4, rows)
        per = lax.dynamic_index_in_dim(per, blk, 2, False)
        per = per.transpose(1, 2, 0)
        return per.reshape(spread, rows * array.shape[0] // 128, 128)

    own_half = lax.dynamic_slice_in_dim(root1, z1 * 2048, 2048, 1)
    both = rows_for(second2, 64, 8)
    send = jnp.concatenate([rows_for(own_half, 32, 16), rows_for(first1, 32, 16), jnp.concatenate([both, both], 0)], 1)
    outward = Beside(send, [lambda v: lax.all_to_all(v, FIRST, 0, 0, tiled=True), None, None, None, lambda v: v])

    second3 = lax.all_gather(second2.reshape(2, 32, 2048), "y1", axis=1).reshape(128, 2048)

    picked3 = pick(wide2, idx_third, 0, 8192) + pick(first3, idx_third, 4096, 8192)
    picked3 = picked3 + pick(second3, idx_third, 6144, 8192)
    res3 = noise3 - dot(picked3.astype(BF), coup_third)
    third3 = solve_chain(full_third, res3, 256, outward)
    got = outward.arrays
    out0 = got[:, :8].reshape(16, 32, 32).transpose(1, 0, 2).reshape(32, 512)
    out1 = got[:, 8:16].reshape(16, 32, 32).transpose(1, 0, 2).reshape(32, 512)
    two = lax.dynamic_slice_in_dim(got[:, 16:], z0 * 8, 8, 0)
    out2 = two.reshape(8, 64, 2, 32).transpose(1, 2, 0, 3).reshape(64, 512)
    three = lax.all_to_all(rows_for(third3, 64, 4), SIDE, 0, 0, tiled=True)
    out3 = three.reshape(4, 64, 4, 32).transpose(1, 2, 0, 3).reshape(64, 512)
    return out0, out1, out2, out3


def solution(mesh):
    fine = Mesh(mesh.devices.reshape((2,) * 7), AXES)
    both = P(LEAF, BLK)
    cross = P(BLK, LEAF)
    list_spec = P(LEAF)
    in_specs = (P(BLK, None), both, cross, both, both, list_spec, cross, both, both, list_spec, cross, both, both, list_spec)
    out_specs = (P(LEAF + BLK, None),) * 4
    return jax.shard_map(local, mesh=fine, in_specs=in_specs, out_specs=out_specs, check_vma=False)
```

```python
import jax
import jax.numpy as jnp
from jax import lax
from jax.sharding import Mesh, PartitionSpec as P

BF = jnp.bfloat16
F32 = jnp.float32
AXES = ("z1", "z0", "y1", "y0", "x0", "x1", "c")
LEAF = ("z1", "z0", "y1", "y0", "x0")
BLK = ("x1", "c")
SIDE = ("y0", "x0")
FIRST = ("z0", "y1", "y0", "x0")
SECOND = ("y1", "y0", "x0")


def dot(left, right):
    return lax.dot_general(left, right, (((1,), (0,)), ((), ())), preferred_element_type=F32)


def swap(array, axes, bits, keep=None):
    count = lax.axis_size(axes)
    route = [(i, i ^ bits) for i in range(count) if keep is None or keep(i)]
    return lax.ppermute(array, axes, route)


def pair_stack(array, axis, at=0):
    other = swap(array, axis, 1)
    low = lax.axis_index(axis) == 0
    return jnp.stack([jnp.where(low, array, other), jnp.where(low, other, array)], at)


def pick(x_t, idx, offset, total, first_entry=0):
    entries = idx.shape[0]
    slack = total - entries
    step = 512
    out = []
    for start in range(0, entries, step):
        low = max(start, offset) - offset
        high = min(start + step + slack, offset + x_t.shape[1]) - offset
        if high <= low:
            out.append(jnp.zeros((x_t.shape[0], step), F32))
            continue
        rows = lax.broadcasted_iota(jnp.int32, (high - low, step), 0) + (low + offset)
        hot = (rows == idx[start : start + step][None, :]).astype(BF)
        out.append(dot(x_t[:, low:high], hot))
    return jnp.concatenate(out, 1)


def bulk_gather(array, axes):
    count = lax.axis_size(axes)
    copies = jnp.broadcast_to(array[None], (count,) + array.shape)
    return lax.all_to_all(copies, axes, 0, 0, tiled=True)


def coupled(picked, coupling, axes):
    count = lax.axis_size(axes)
    rows, tile = coupling.shape
    samples = picked.shape[0]
    send = picked.astype(BF).reshape(samples, count, rows).transpose(1, 0, 2)
    got = lax.all_to_all(send, axes, 0, 0, tiled=True).reshape(count * samples, rows)
    part = dot(got, coupling).astype(BF).reshape(count, samples, tile)
    back = lax.all_to_all(part, axes, 0, 0, tiled=True)
    return jnp.sum(back.astype(F32), 0)


class Beside:
    def __init__(self, arrays, stages):
        self.arrays = arrays
        self.stages = list(stages)

    def step(self, value):
        if self.stages:
            stage = self.stages.pop(0)
            if stage is not None:
                value, self.arrays = lax.optimization_barrier((value, self.arrays))
                self.arrays = stage(self.arrays)
        return value


class Both:
    def __init__(self, *parts):
        self.parts = parts

    def step(self, value):
        for part in self.parts:
            value = part.step(value)
        return value


def root_rows(block_root):
    c = lax.axis_index("c")
    x0 = lax.axis_index("x0")
    halves = block_root.reshape(128, 2, 512)
    kept = lax.dynamic_index_in_dim(halves, x0, 1, False)
    gone = lax.dynamic_index_in_dim(halves, 1 - x0, 1, False)
    kept = lax.ppermute(kept, ("x0", "c"), [(0, 0), (1, 2), (2, 1), (3, 3)])
    gone = lax.ppermute(gone, ("x0", "c"), [(0, 1), (1, 3), (2, 0), (3, 2)])
    even = jnp.where(c == 0, kept, gone)
    odd = jnp.where(c == 0, gone, kept)
    rows = jnp.concatenate([even, odd], 0)
    return rows


def solve_root(noise_root, weights):
    y = lax.axis_index(("y1", "y0"))
    z0, x0, c = (lax.axis_index(a) for a in ("z0", "x0", "c"))
    tile = lax.axis_index("x1") * 2 + x0
    sample0 = (z0 * 4 + y) * 64

    def share(half):
        return lax.all_gather(half, "c", axis=1, tiled=True)

    mine = lax.dynamic_slice_in_dim(noise_root, sample0, 64, 1).T
    held = lax.dynamic_slice_in_dim(mine, c * 512, 512, 1)
    sent = lax.dynamic_slice_in_dim(mine, (1 - c) * 512, 512, 1)
    rest = jnp.where(c == x0, held, swap(sent, "c", 1))
    diagonal = lax.dynamic_slice_in_dim(weights, tile * 1024, 1024, 0)
    solved = [None] * 4
    for t in (3, 2, 1, 0):
        own = dot(share(rest.astype(BF)), diagonal).astype(BF)
        own = jnp.where(tile == t, own, jnp.zeros(own.shape, BF))
        half = own
        for bits in (1, 2, 3):
            half = half + swap(own, ("x0", "x1"), bits, lambda i: i == (t & 1) * 2 + (t >> 1))
        solved[t] = share(half)
        if t:
            rest = rest - dot(solved[t], weights[t * 1024 : (t + 1) * 1024])
    return jnp.concatenate(solved, 1)


def solve_chain(block, residual, tile, beside):
    blk = lax.axis_index(BLK)
    x1 = lax.axis_index("x1")
    inverse = lax.dynamic_slice_in_dim(block, blk * tile, tile, 0)
    below = lax.dynamic_slice_in_dim(block, (2 * x1 + 1) * tile, tile, 0)

    def chip_solve(rest):
        rest = beside.step(rest)
        later = lax.all_gather(dot(rest.astype(BF), inverse).astype(BF), "c")[1]
        rest = rest - dot(later, below)
        rest = beside.step(rest)
        sooner = lax.all_gather(dot(rest.astype(BF), inverse).astype(BF), "c")[0]
        return lax.all_gather(jnp.concatenate([sooner, later], 1), "x1")

    late = chip_solve(residual)[1]
    early = chip_solve(residual - dot(late, block[2 * tile :]))[0]
    early = beside.step(early)
    return jnp.concatenate([early, late], 1)


def local(noise_root, block_root, noise_first, block_first, coupling_first, structure_first,
          noise_second, block_second, coupling_second, structure_second,
          noise_third, block_third, coupling_third, structure_third):
    z1, z0, y1, y0, x0 = (lax.axis_index(a) for a in LEAF)
    blk = lax.axis_index(BLK)

    lists = jnp.concatenate([structure_first, structure_second, structure_third])
    for place, axis in enumerate(("z0", "y1", "y0")):
        lists = pair_stack(lists, axis, place)

    def along(axis):
        return lambda pair: tuple(pair_stack(array, axis) for array in pair)

    rows, lists = lax.optimization_barrier((root_rows(block_root), lists))
    weights = bulk_gather(rows, ("z1", "z0", "y1", "y0")).reshape(4096, 512)
    lists = pair_stack(lists, "x0", 3).reshape(16, 1344)
    idx_first = lists[:, :192].reshape(3072)
    idx_second = lax.dynamic_slice(lists, (z0 * 8, 192), (8, 384)).reshape(3072)
    idx_third = lax.dynamic_slice(lists, (z0 * 8 + y1 * 4, 576), (4, 768)).reshape(3072)

    noise1 = noise_first.T
    halves = noise_second.T.reshape(2, 32, 512)
    a = y1
    first_route, second_route = [], []
    for s in range(8):
        p, q, r = s >> 2, s >> 1 & 1, s & 1
        first_route.append((s, q * 4 + r * 2 + p))
        second_route.append((s, q * 4 + r * 2 + 1 - p))
    same = lax.ppermute(lax.dynamic_index_in_dim(halves, a, 0, False), SECOND, first_route)
    cross = lax.ppermute(lax.dynamic_index_in_dim(halves, 1 - a, 0, False), SECOND, second_route)
    noise2 = jnp.concatenate([jnp.where(x0 == 0, same, cross), jnp.where(x0 == 0, cross, same)], 0)
    quarters = noise_third.T.reshape(4, 32, 256)
    me = y0 * 2 + x0
    pieces = []
    for bits in (0, 1, 2, 3):
        piece = lax.dynamic_index_in_dim(quarters, me ^ bits, 0, False)
        pieces.append(piece if bits == 0 else swap(piece, SIDE, bits))
    pieces = jnp.stack(pieces, 0)
    noise3 = jnp.concatenate([lax.dynamic_index_in_dim(pieces, me ^ t, 0, False) for t in range(4)], 0)

    full_first = lax.all_gather(block_first, FIRST, axis=0, tiled=True)
    full_second = lax.all_gather(block_second, SECOND, axis=0, tiled=True)
    ready = (weights, idx_first, idx_second, idx_third, noise1, noise2, noise3)
    weights, idx_first, idx_second, idx_third, noise1, noise2, noise3 = lax.optimization_barrier(ready)

    root = solve_root(noise_root, weights)
    root1 = lax.dynamic_slice_in_dim(root, x0 * 32, 32, 0)

    def widen(array):
        return pair_stack(array.reshape(2, 32, array.shape[1]), "y1", 1).reshape(128, array.shape[1])

    res1 = noise1 - coupled(pick(root1, idx_first, 0, 4096), coupling_first, FIRST)
    root2 = pair_stack(root1, "z0").reshape(64, 4096)
    wide2, res1 = lax.optimization_barrier((root2, res1))
    wide2 = widen(wide2)
    first1 = solve_chain(full_first, res1, 512, Beside((), []))
    wide2, first1 = lax.optimization_barrier((wide2, first1))
    first2 = lax.all_gather(first1, "z0").reshape(64, 2048)

    third_stages = Beside((block_third, coupling_third), [along("x0"), None, along("y0"), None, None, lambda v: v])
    first2 = third_stages.step(first2)
    picked2 = pick(root2, idx_second, 0, 6144) + pick(first2, idx_second, 4096, 6144)
    res2 = noise2 - coupled(picked2, coupling_second, SECOND)
    widening = Beside(first2, [None, widen, None, None, lambda v: v])
    second2 = solve_chain(full_second, res2, 512, Both(third_stages, widening))
    full_third, coup_third = (array.reshape(-1, 256) for array in third_stages.arrays)

    def rows_for(array, rows, spread):
        per = array.reshape(array.shape[0], spread, 4, rows)
        per = lax.dynamic_index_in_dim(per, blk, 2, False)
        per = per.transpose(1, 2, 0)
        return per.reshape(spread, rows * array.shape[0] // 128, 128)

    own_half = lax.dynamic_slice_in_dim(root1, z1 * 2048, 2048, 1)
    both = rows_for(second2, 64, 8)
    send = jnp.concatenate([rows_for(own_half, 32, 16), rows_for(first1, 32, 16), jnp.concatenate([both, both], 0)], 1)
    outward = Beside(send, [lambda v: lax.all_to_all(v, FIRST, 0, 0, tiled=True), None, None, None, lambda v: v])

    first3 = widening.arrays
    second3 = lax.all_gather(second2.reshape(2, 32, 2048), "y1", axis=1).reshape(128, 2048)

    picked3 = pick(wide2, idx_third, 0, 8192) + pick(first3, idx_third, 4096, 8192)
    picked3 = picked3 + pick(second3, idx_third, 6144, 8192)
    res3 = noise3 - dot(picked3.astype(BF), coup_third)
    third3 = solve_chain(full_third, res3, 256, outward)
    got = outward.arrays
    out0 = got[:, :8].reshape(16, 32, 32).transpose(1, 0, 2).reshape(32, 512)
    out1 = got[:, 8:16].reshape(16, 32, 32).transpose(1, 0, 2).reshape(32, 512)
    two = lax.dynamic_slice_in_dim(got[:, 16:], z0 * 8, 8, 0)
    out2 = two.reshape(8, 64, 2, 32).transpose(1, 2, 0, 3).reshape(64, 512)
    three = third3.reshape(128, 4, 4, 64)
    three = lax.dynamic_index_in_dim(three, blk, 2, False).transpose(1, 0, 2)
    three = lax.all_to_all(three, SIDE, 0, 0, tiled=True)
    out3 = three.reshape(4, 4, 32, 64).transpose(1, 0, 2, 3).reshape(512, 64).T
    return out0, out1, out2, out3


def solution(mesh):
    fine = Mesh(mesh.devices.reshape((2,) * 7), AXES)
    both = P(LEAF, BLK)
    cross = P(BLK, LEAF)
    list_spec = P(LEAF)
    in_specs = (P(BLK, None), both, cross, both, both, list_spec, cross, both, both, list_spec, cross, both, both, list_spec)
    out_specs = (P(LEAF + BLK, None),) * 4
    return jax.shard_map(local, mesh=fine, in_specs=in_specs, out_specs=out_specs, check_vma=False)
```

```python
import jax
import jax.numpy as jnp
from jax import lax
from jax.sharding import Mesh, PartitionSpec as P

BF = jnp.bfloat16
F32 = jnp.float32
AXES = ("z1", "z0", "y1", "y0", "x0", "x1", "c")
LEAF = ("z1", "z0", "y1", "y0", "x0")
BLK = ("x1", "c")
SIDE = ("y0", "x0")
FIRST = ("z0", "y1", "y0", "x0")
SECOND = ("y1", "y0", "x0")


def dot(left, right):
    return lax.dot_general(left, right, (((1,), (0,)), ((), ())), preferred_element_type=F32)


def swap(array, axes, bits, keep=None):
    count = lax.axis_size(axes)
    route = [(i, i ^ bits) for i in range(count) if keep is None or keep(i)]
    return lax.ppermute(array, axes, route)


def pair_stack(array, axis, at=0):
    other = swap(array, axis, 1)
    low = lax.axis_index(axis) == 0
    return jnp.stack([jnp.where(low, array, other), jnp.where(low, other, array)], at)


def pick(x_t, idx, offset, total, first_entry=0):
    entries = idx.shape[0]
    slack = total - entries
    step = 512
    out = []
    for start in range(0, entries, step):
        low = max(start, offset) - offset
        high = min(start + step + slack, offset + x_t.shape[1]) - offset
        if high <= low:
            out.append(jnp.zeros((x_t.shape[0], step), F32))
            continue
        rows = lax.broadcasted_iota(jnp.int32, (high - low, step), 0) + (low + offset)
        hot = (rows == idx[start : start + step][None, :]).astype(BF)
        out.append(dot(x_t[:, low:high], hot))
    return jnp.concatenate(out, 1)


def bulk_gather(array, axes):
    count = lax.axis_size(axes)
    copies = jnp.broadcast_to(array[None], (count,) + array.shape)
    return lax.all_to_all(copies, axes, 0, 0, tiled=True)


def coupled(picked, coupling, axes):
    count = lax.axis_size(axes)
    rows, tile = coupling.shape
    samples = picked.shape[0]
    send = picked.astype(BF).reshape(samples, count, rows).transpose(1, 0, 2)
    got = lax.all_to_all(send, axes, 0, 0, tiled=True).reshape(count * samples, rows)
    part = dot(got, coupling).astype(BF).reshape(count, samples, tile)
    back = lax.all_to_all(part, axes, 0, 0, tiled=True)
    return jnp.sum(back.astype(F32), 0)


class Beside:
    def __init__(self, arrays, stages):
        self.arrays = arrays
        self.stages = list(stages)

    def step(self, value):
        if self.stages:
            stage = self.stages.pop(0)
            if stage is not None:
                value, self.arrays = lax.optimization_barrier((value, self.arrays))
                self.arrays = stage(self.arrays)
        return value


def root_rows(block_root):
    c = lax.axis_index("c")
    x0 = lax.axis_index("x0")
    halves = block_root.reshape(128, 2, 512)
    kept = lax.dynamic_index_in_dim(halves, x0, 1, False)
    gone = lax.dynamic_index_in_dim(halves, 1 - x0, 1, False)
    kept = lax.ppermute(kept, ("x0", "c"), [(0, 0), (1, 2), (2, 1), (3, 3)])
    gone = lax.ppermute(gone, ("x0", "c"), [(0, 1), (1, 3), (2, 0), (3, 2)])
    even = jnp.where(c == 0, kept, gone)
    odd = jnp.where(c == 0, gone, kept)
    rows = jnp.concatenate([even, odd], 0)
    return rows


def solve_root(noise_root, weights):
    y = lax.axis_index(("y1", "y0"))
    z0, x0, c = (lax.axis_index(a) for a in ("z0", "x0", "c"))
    tile = lax.axis_index("x1") * 2 + x0
    sample0 = (z0 * 4 + y) * 64

    def share(half):
        return lax.all_gather(half, "c", axis=1, tiled=True)

    mine = lax.dynamic_slice_in_dim(noise_root, sample0, 64, 1).T
    held = lax.dynamic_slice_in_dim(mine, c * 512, 512, 1)
    sent = lax.dynamic_slice_in_dim(mine, (1 - c) * 512, 512, 1)
    rest = jnp.where(c == x0, held, swap(sent, "c", 1))
    diagonal = lax.dynamic_slice_in_dim(weights, tile * 1024, 1024, 0)
    solved = [None] * 4
    for t in (3, 2, 1, 0):
        own = dot(share(rest.astype(BF)), diagonal).astype(BF)
        own = jnp.where(tile == t, own, jnp.zeros(own.shape, BF))
        half = own
        for bits in (1, 2, 3):
            half = half + swap(own, ("x0", "x1"), bits, lambda i: i == (t & 1) * 2 + (t >> 1))
        solved[t] = share(half)
        if t:
            rest = rest - dot(solved[t], weights[t * 1024 : (t + 1) * 1024])
    return jnp.concatenate(solved, 1)


def solve_chain(block, residual, tile, beside):
    blk = lax.axis_index(BLK)
    x1 = lax.axis_index("x1")
    inverse = lax.dynamic_slice_in_dim(block, blk * tile, tile, 0)
    below = lax.dynamic_slice_in_dim(block, (2 * x1 + 1) * tile, tile, 0)

    def chip_solve(rest):
        rest = beside.step(rest)
        later = lax.all_gather(dot(rest.astype(BF), inverse).astype(BF), "c")[1]
        rest = rest - dot(later, below)
        rest = beside.step(rest)
        sooner = lax.all_gather(dot(rest.astype(BF), inverse).astype(BF), "c")[0]
        return lax.all_gather(jnp.concatenate([sooner, later], 1), "x1")

    late = chip_solve(residual)[1]
    early = chip_solve(residual - dot(late, block[2 * tile :]))[0]
    early = beside.step(early)
    return jnp.concatenate([early, late], 1)


def local(noise_root, block_root, noise_first, block_first, coupling_first, structure_first,
          noise_second, block_second, coupling_second, structure_second,
          noise_third, block_third, coupling_third, structure_third):
    z1, z0, y1, y0, x0 = (lax.axis_index(a) for a in LEAF)
    blk = lax.axis_index(BLK)

    lists = jnp.concatenate([structure_first, structure_second, structure_third])
    for place, axis in enumerate(("z0", "y1", "y0")):
        lists = pair_stack(lists, axis, place)

    def along(axis):
        return lambda pair: tuple(pair_stack(array, axis) for array in pair)

    rows, lists = lax.optimization_barrier((root_rows(block_root), lists))
    weights = bulk_gather(rows, ("z1", "z0", "y1", "y0")).reshape(4096, 512)
    lists = pair_stack(lists, "x0", 3).reshape(16, 1344)
    idx_first = lists[:, :192].reshape(3072)
    idx_second = lax.dynamic_slice(lists, (z0 * 8, 192), (8, 384)).reshape(3072)
    idx_third = lax.dynamic_slice(lists, (z0 * 8 + y1 * 4, 576), (4, 768)).reshape(3072)

    noise1 = noise_first.T
    halves = noise_second.T.reshape(2, 32, 512)
    a = y1
    first_route, second_route = [], []
    for s in range(8):
        p, q, r = s >> 2, s >> 1 & 1, s & 1
        first_route.append((s, q * 4 + r * 2 + p))
        second_route.append((s, q * 4 + r * 2 + 1 - p))
    same = lax.ppermute(lax.dynamic_index_in_dim(halves, a, 0, False), SECOND, first_route)
    cross = lax.ppermute(lax.dynamic_index_in_dim(halves, 1 - a, 0, False), SECOND, second_route)
    noise2 = jnp.concatenate([jnp.where(x0 == 0, same, cross), jnp.where(x0 == 0, cross, same)], 0)
    quarters = noise_third.T.reshape(4, 32, 256)
    me = y0 * 2 + x0
    pieces = []
    for bits in (0, 1, 2, 3):
        piece = lax.dynamic_index_in_dim(quarters, me ^ bits, 0, False)
        pieces.append(piece if bits == 0 else swap(piece, SIDE, bits))
    pieces = jnp.stack(pieces, 0)
    noise3 = jnp.concatenate([lax.dynamic_index_in_dim(pieces, me ^ t, 0, False) for t in range(4)], 0)

    full_first = lax.all_gather(block_first, FIRST, axis=0, tiled=True)
    full_second = lax.all_gather(block_second, SECOND, axis=0, tiled=True)
    ready = (weights, idx_first, idx_second, idx_third, noise1, noise2, noise3)
    weights, idx_first, idx_second, idx_third, noise1, noise2, noise3 = lax.optimization_barrier(ready)

    root = solve_root(noise_root, weights)
    root1 = lax.dynamic_slice_in_dim(root, x0 * 32, 32, 0)

    def widen(array):
        return pair_stack(array.reshape(2, 32, array.shape[1]), "y1", 1).reshape(128, array.shape[1])

    res1 = noise1 - coupled(pick(root1, idx_first, 0, 4096), coupling_first, FIRST)
    root2 = pair_stack(root1, "z0").reshape(64, 4096)
    wide2, res1 = lax.optimization_barrier((root2, res1))
    wide2 = widen(wide2)
    first1 = solve_chain(full_first, res1, 512, Beside((), []))
    wide2, first1 = lax.optimization_barrier((wide2, first1))
    first2 = lax.all_gather(first1, "z0").reshape(64, 2048)

    third_stages = Beside((block_third, coupling_third), [along("x0"), None, along("y0"), None, None, lambda v: v])
    first2 = third_stages.step(first2)
    picked2 = pick(root2, idx_second, 0, 6144) + pick(first2, idx_second, 4096, 6144)
    res2 = noise2 - coupled(picked2, coupling_second, SECOND)
    second2 = solve_chain(full_second, res2, 512, third_stages)
    full_third, coup_third = (array.reshape(-1, 256) for array in third_stages.arrays)

    def rows_for(array, rows, spread):
        per = array.reshape(array.shape[0], spread, 4, rows)
        per = lax.dynamic_index_in_dim(per, blk, 2, False)
        per = per.transpose(1, 2, 0)
        return per.reshape(spread, rows * array.shape[0] // 128, 128)

    own_half = lax.dynamic_slice_in_dim(root1, z1 * 2048, 2048, 1)
    both = rows_for(second2, 64, 8)
    send = jnp.concatenate([rows_for(own_half, 32, 16), rows_for(first1, 32, 16), jnp.concatenate([both, both], 0)], 1)
    outward = Beside(send, [lambda v: lax.all_to_all(v, FIRST, 0, 0, tiled=True), None, None, None, lambda v: v])

    first3 = widen(first2)
    second3 = lax.all_gather(second2.reshape(2, 32, 2048), "y1", axis=1).reshape(128, 2048)

    picked3 = pick(wide2, idx_third, 0, 8192) + pick(first3, idx_third, 4096, 8192)
    picked3 = picked3 + pick(second3, idx_third, 6144, 8192)
    res3 = noise3 - dot(picked3.astype(BF), coup_third)
    third3 = solve_chain(full_third, res3, 256, outward)
    got = outward.arrays
    out0 = got[:, :8].reshape(16, 32, 32).transpose(1, 0, 2).reshape(32, 512)
    out1 = got[:, 8:16].reshape(16, 32, 32).transpose(1, 0, 2).reshape(32, 512)
    two = lax.dynamic_slice_in_dim(got[:, 16:], z0 * 8, 8, 0)
    out2 = two.reshape(8, 64, 2, 32).transpose(1, 2, 0, 3).reshape(64, 512)
    three = lax.all_to_all(rows_for(third3, 64, 4), SIDE, 0, 0, tiled=True)
    out3 = three.reshape(4, 64, 4, 32).transpose(1, 2, 0, 3).reshape(64, 512)
    return out0, out1, out2, out3


def solution(mesh):
    fine = Mesh(mesh.devices.reshape((2,) * 7), AXES)
    both = P(LEAF, BLK)
    cross = P(BLK, LEAF)
    list_spec = P(LEAF)
    in_specs = (P(BLK, None), both, cross, both, both, list_spec, cross, both, both, list_spec, cross, both, both, list_spec)
    out_specs = (P(LEAF + BLK, None),) * 4
    return jax.shard_map(local, mesh=fine, in_specs=in_specs, out_specs=out_specs, check_vma=False)
```
